32 devices in a mesh: groups: 2 (over x), blk: 16 (over z, y, core).
Axes of the slice: x: 2, y: 2, z: 4, core: 2. Of those that a mesh axis runs over, the one named last changes fastest.
Arguments:
- flow: float32 [16384, 2560], P(('groups', 'blk')), parts along dimension 0, as said below
- occupancy: int32 [32, 5], P(('groups', 'blk')), parts along dimension 0, may hold values from 0 to 1, as said below
Outputs:
- clustered: float32 [16384, 2560], P(('groups', 'blk')), parts along dimension 0
The draws below stay inside these ranges and needn't reach their ends.
There are 2 independent parts, one for each index of `groups`. The reference program is written for one: setup_inputs(seed, part) draws one part's arguments, and reference() takes and returns one part's arrays. A program takes and returns all parts, laid end to end along the dimension named above; each array names one. Nothing has to cross between parts.
Inputs may be any that keep to these rules, and one draw needn't show every extreme that they name: `occupancy`: slot 2 (the diagonal tile) of every row block is occupied; some row blocks have every slot occupied. `flow`: entries are positive.
All inputs are finite; a program needn't handle non-finite values.
Results may differ from the reference program's by a relative error of at most 0.0003.
Values sent between devices are 32-bit elements; how exact they have to be, the bound alone decides.
A program may use at most 64 MiB of HBM per device.

```python
import math
import jax
import jax.numpy as jnp
from jax import lax

BS = 512
R = 2
BLOCKS = 16
NODES = 8192
SPAN = 5
WIN = 2560


def draw_flow(key, part):
    first, second, third = jax.random.split(jax.random.fold_in(key, 11), 3)
    entries = jnp.exp(jax.random.uniform(first, (NODES, WIN), jnp.float32, math.log(0.1), 0.0))
    row_scale = jnp.exp(jax.random.uniform(second, (NODES, 1), jnp.float32, 0.0, math.log(10.0)))
    col_scale = jnp.exp(jax.random.uniform(third, (1, WIN), jnp.float32, 0.0, math.log(10.0)))
    return (entries * row_scale * col_scale * 0.1).astype(jnp.float32)


def draw_occupancy(key, part):
    first, second = jax.random.split(jax.random.fold_in(key, 23), 2)
    heavy = jax.random.randint(first, (BLOCKS, 1), 0, 4) == 0
    heavy = heavy.at[0, 0].set(True)
    others = jax.random.randint(second, (BLOCKS, SPAN), 0, 4) == 0
    filled = jnp.where(heavy | others, 1, 0).astype(jnp.int32)
    return filled.at[:, R].set(1)


def setup_inputs(seed: int = 0, part: int = 0) -> dict:
    seeds = jax.random.split(jax.random.key(seed), 3)
    part_keys = jax.random.split(jax.random.fold_in(seeds[2], part), 3)
    return {
        "flow": draw_flow(jax.random.fold_in(jax.random.fold_in(seeds[2], part), 71), part),
        "occupancy": draw_occupancy(jax.random.fold_in(jax.random.fold_in(seeds[2], part), 71), part),
    }


def reference(flow, occupancy):
    width = BS
    span = 2 * R + 1
    count = BLOCKS
    tiles = flow.reshape(count, width, span, width) * occupancy.astype(jnp.float32)[:, None, :, None]

    def one_row(index):
        left_row = lax.dynamic_index_in_dim(tiles, index, 0, keepdims=False)
        total = jnp.zeros((width, span, width), jnp.float32)
        for offset in range(-R, R + 1):
            source = ((index + offset) % count).astype(jnp.int32)
            window = lax.dynamic_index_in_dim(tiles, source, 0, keepdims=False)
            left = left_row[:, offset + R]
            for target in range(-R, R + 1):
                slot = target - offset + R
                if slot >= 0 and slot < span:
                    term = jnp.dot(left, window[:, slot], precision=lax.Precision.HIGHEST, preferred_element_type=jnp.float32)
                    total = total.at[:, target + R].add(term)
        return total

    totals = lax.map(one_row, jnp.arange(count, dtype=jnp.int32))
    expanded = totals * occupancy.astype(jnp.float32)[:, None, :, None]
    inflated = expanded * expanded
    parts = jnp.sum(inflated, axis=1)
    colsum = jnp.zeros((count, width), jnp.float32)
    for target in range(-R, R + 1):
        colsum = colsum + jnp.roll(parts[:, target + R], target, axis=0)
    near = jnp.stack([jnp.roll(colsum, -target, axis=0) for target in range(-R, R + 1)], axis=1)
    clustered = width * inflated / near[:, None, :, :]
    return clustered.reshape(count * width, span * width)
```

```python
import functools

import jax
import jax.numpy as jnp
from jax import lax
from jax.experimental import pallas as pl
from jax.experimental.pallas import tpu as pltpu
from jax.sharding import PartitionSpec as P

MESH = pl.DeviceIdType.MESH
SPAN = 5
REACH = 2
NEAR = 4
WINDOW = 2


def place(offset, slot):
    return {1: 0, 2: 4, -1: 6, -2: 9}[offset] + slot


OUTER_SENDS = (
    (3, 2, place(2, 1)),
    (2, 2, place(2, 2)),
    (1, -1, place(-1, 3)),
    (0, -1, place(-1, 4)),
    (4, 2, place(2, 0)),
)
INNER_SENDS = (
    (2, 1, place(1, 2)),
    (1, 1, place(1, 3)),
    (4, 1, place(1, 0)),
    (3, 1, place(1, 1)),
    (0, -2, place(-2, 4)),
)
OUTER_STEPS = ((2, 2), (-2, 2), (-1, 1), (-2, 3), (-1, 2), (-1, 3), (2, 0), (-1, 4), (2, 1), (-2, 4))
INNER_STEPS = ((1, 2), (2, 1), (1, 3), (2, 2), (1, 0), (-2, 2), (1, 1), (-2, 3), (2, 0), (-2, 4))
OUTER_FORWARDS = {
    (-1, 2): ((1, place(-2, 2)),),
    (-1, 3): ((1, place(-2, 3)),),
    (-1, 4): ((1, place(-2, 4)),),
}
INNER_FORWARDS = {
    (1, 2): ((3, place(-2, 2)), (-1, place(2, 2))),
    (2, 1): ((3, place(-1, 1)),),
    (1, 3): ((3, place(-2, 3)),),
    (2, 2): ((3, place(-1, 2)),),
    (1, 0): ((-1, place(2, 0)),),
    (1, 1): ((-1, place(2, 1)),),
}
COMPLETE = {1: (4, 3), 3: (0, 4), 5: (1, 0), 8: (3, 1), 9: (2, 2)}
NEXT_SEND = {0: 2, 2: 3, 4: 4}


def body(
    count,
    width,
    flow_ref,
    occ_ref,
    infl_ref,
    near_ref,
    own,
    high,
    low,
    recv,
    acc,
    right_high,
    right_low,
    parts,
    load_sem,
    store_sem,
    send_sem,
    recv_sem,
    part_send_sem,
    part_recv_sem,
):
    me = lax.axis_index("blk")
    spot = lax.rem(me, 4)
    outer = jnp.logical_or(spot == 0, spot == 3)
    sign = jnp.where(spot < 2, 1, -1)

    def pick(a, b):
        return a if isinstance(a, int) and a == b else jnp.where(outer, a, b)

    def peer(offset):
        return {"blk": lax.rem(me + sign * offset + count, count)}

    def absolute(slot):
        return REACH + sign * (slot - REACH)

    def columns(slot):
        return pl.ds(pl.multiple_of(absolute(slot) * width, width), width)

    def load(slot):
        return pltpu.make_async_copy(flow_ref.at[:, columns(slot)], own.at[slot], load_sem.at[slot])

    def remote(source, target, where, sem):
        return pltpu.make_async_remote_copy(
            src_ref=source,
            dst_ref=recv.at[where],
            send_sem=send_sem.at[sem],
            recv_sem=recv_sem.at[where],
            device_id=target,
            device_id_type=MESH,
        )

    own_slots = [pick(OUTER_SENDS[t][0], INNER_SENDS[t][0]) for t in range(SPAN)]
    for t in range(SPAN):
        load(own_slots[t]).start()

    barrier = pltpu.get_barrier_semaphore()
    for distance in range(1, NEAR + 1):
        for offset in (distance, -distance):
            pl.semaphore_signal(barrier, inc=1, device_id=peer(offset), device_id_type=MESH)
    pl.semaphore_wait(barrier, 2 * NEAR)

    rows = 64

    def prepare(slot):
        load(slot).wait()
        factor = occ_ref[0, absolute(slot)].astype(jnp.float32)

        @pl.loop(0, width // rows)
        def _(r):
            at = pl.ds(pl.multiple_of(r * rows, rows), rows)
            masked = own[slot, at, :] * factor
            own[slot, at, :] = masked
            top = masked.astype(jnp.bfloat16)
            high[slot, at, :] = top
            low[slot, at, :] = (masked - top.astype(jnp.float32)).astype(jnp.bfloat16)

    def send(t):
        source, offset, where = (pick(a, b) for a, b in zip(OUTER_SENDS[t], INNER_SENDS[t]))
        return remote(own.at[source], peer(offset), where, t)

    def local_send(q):
        return remote(own.at[pick(q + 1, q)], peer(pick(1, -1)), pick(place(-1, q + 1), place(1, q)), SPAN + q)

    for t in range(SPAN):
        prepare(own_slots[t])
        if t < WINDOW:
            send(t).start()
    for q in range(SPAN - 1):
        local_send(q).start()

    half = width // 2

    def multiply(left, get_high, get_low, out, first):
        @pl.loop(0, 2)
        def _(c):
            at = pl.ds(pl.multiple_of(c * half, half), half)
            term = functools.partial(jnp.dot, preferred_element_type=jnp.float32)
            total = term(high[left], get_high(at))
            total += term(high[left], get_low(at)) + term(low[left], get_high(at))
            if first:
                acc[out, :, at] = total
            else:
                acc[out, :, at] += total

    @pl.loop(0, SPAN)
    def _(slot):
        multiply(REACH, lambda at: high[slot, :, at], lambda at: low[slot, :, at], slot, True)

    def arrived(where):
        remote(recv.at[where], peer(1), where, 0).wait_recv()

    def add(where, left, out):
        @pl.loop(0, width // rows)
        def _(r):
            at = pl.ds(pl.multiple_of(r * rows, rows), rows)
            value = recv[where, at, :]
            top = value.astype(jnp.bfloat16)
            right_high[at, :] = top
            right_low[at, :] = (value - top.astype(jnp.float32)).astype(jnp.bfloat16)

        multiply(left, lambda at: right_high[:, at], lambda at: right_low[:, at], out, False)

    @pl.loop(0, SPAN - 1)
    def _(q):
        where = jnp.where(outer, q, place(-1, 1) + q)
        arrived(where)
        add(where, pick(3, 1), jnp.where(outer, q + 1, q))

    def store(slot):
        return pltpu.make_async_copy(acc.at[slot], infl_ref.at[:, columns(slot)], store_sem.at[slot])

    parts[NEAR] = jnp.zeros((8, width), jnp.float32)

    def complete(slot):
        factor = occ_ref[0, absolute(slot)].astype(jnp.float32)

        def some(r, total):
            at = pl.ds(pl.multiple_of(r * rows, rows), rows)
            expanded = acc[slot, at, :] * factor
            inflated = expanded * expanded
            acc[slot, at, :] = inflated
            return total + jnp.sum(inflated.reshape(rows // 8, 8, width), axis=0)

        total = lax.fori_loop(0, width // rows, some, jnp.zeros((8, width), jnp.float32))
        parts[NEAR, pl.ds(absolute(slot), 1), :] = jnp.sum(total, axis=0, keepdims=True)
        store(slot).start()

    def forwards(table, tile):
        found = []
        order = [(t, f) for t in table for f in table[t]]
        for number, (t, (offset, where)) in enumerate(order):
            if t == tile:
                found.append(remote(recv.at[place(*t)], peer(offset), where, 2 * SPAN - 1 + number))
        return found

    for step in range(10):
        far, near = OUTER_STEPS[step], INNER_STEPS[step]
        if step in NEXT_SEND:
            t = NEXT_SEND[step]
            send(t - WINDOW).wait_send()
            send(t).start()
        where = pick(place(*far), place(*near))
        arrived(where)
        if far in OUTER_FORWARDS:
            @pl.when(outer)
            def _():
                for copy in forwards(OUTER_FORWARDS, far):
                    copy.start()
        if near in INNER_FORWARDS:
            @pl.when(jnp.logical_not(outer))
            def _():
                for copy in forwards(INNER_FORWARDS, near):
                    copy.start()
        add(where, pick(far[0] + REACH, near[0] + REACH), pick(sum(far), sum(near)))
        if step in COMPLETE:
            complete(pick(*COMPLETE[step]))

    def part(offset):
        target = {"blk": lax.rem(me + offset + count, count)}
        return pltpu.make_async_remote_copy(
            src_ref=parts.at[NEAR],
            dst_ref=parts.at[NEAR - offset],
            send_sem=part_send_sem.at[NEAR - offset],
            recv_sem=part_recv_sem.at[NEAR - offset],
            device_id=target,
            device_id_type=MESH,
        )

    reaches = [offset for offset in range(-NEAR, NEAR + 1) if offset != 0]
    for offset in reaches:
        part(offset).start()
    for offset in reaches:
        part(offset).wait_recv()
    for slot in range(SPAN):
        total = parts[slot, pl.ds(SPAN - 1, 1), :]
        for d in range(slot - REACH * 2 + 1, slot + 1):
            total = total + parts[NEAR + d, pl.ds(slot - d, 1), :]
        near_ref[:, slot * width : (slot + 1) * width] = total

    for offset in reaches:
        part(offset).wait_send()
    for slot in range(SPAN):
        store(slot).wait()
    for t in range(SPAN - WINDOW, SPAN):
        send(t).wait_send()
    for q in range(SPAN - 1):
        local_send(q).wait_send()

    @pl.when(outer)
    def _():
        for tile in OUTER_FORWARDS:
            for copy in forwards(OUTER_FORWARDS, tile):
                copy.wait_send()

    @pl.when(jnp.logical_not(outer))
    def _():
        for tile in INNER_FORWARDS:
            for copy in forwards(INNER_FORWARDS, tile):
                copy.wait_send()


def per_device(count, flow, occupancy):
    width = flow.shape[0]
    tile = (width, width)
    places = 14
    inflated, near = pl.pallas_call(
        functools.partial(body, count, width),
        out_shape=(
            jax.ShapeDtypeStruct(flow.shape, jnp.float32),
            jax.ShapeDtypeStruct((1, flow.shape[1]), jnp.float32),
        ),
        in_specs=[
            pl.BlockSpec(memory_space=pl.ANY),
            pl.BlockSpec(memory_space=pltpu.SMEM),
        ],
        out_specs=(
            pl.BlockSpec(memory_space=pl.ANY),
            pl.BlockSpec(memory_space=pltpu.VMEM),
        ),
        scratch_shapes=[
            pltpu.VMEM((SPAN, *tile), jnp.float32),
            pltpu.VMEM((SPAN, *tile), jnp.bfloat16),
            pltpu.VMEM((SPAN, *tile), jnp.bfloat16),
            pltpu.VMEM((places, *tile), jnp.float32),
            pltpu.VMEM((SPAN, *tile), jnp.float32),
            pltpu.VMEM(tile, jnp.bfloat16),
            pltpu.VMEM(tile, jnp.bfloat16),
            pltpu.VMEM((2 * NEAR + 1, 8, width), jnp.float32),
            pltpu.SemaphoreType.DMA((SPAN,)),
            pltpu.SemaphoreType.DMA((SPAN,)),
            pltpu.SemaphoreType.DMA((2 * SPAN - 1 + 8,)),
            pltpu.SemaphoreType.DMA((places,)),
            pltpu.SemaphoreType.DMA((2 * NEAR + 1,)),
            pltpu.SemaphoreType.DMA((2 * NEAR + 1,)),
        ],
        compiler_params=pltpu.CompilerParams(
            collective_id=0, has_side_effects=True, vmem_limit_bytes=48 * 1024 * 1024
        ),
        name="expand",
    )(flow, occupancy)
    return width * inflated / near


def solution(mesh):
    placed = (P(("groups", "blk"), None), P(("groups", "blk"), None))
    return jax.shard_map(
        functools.partial(per_device, mesh.shape["blk"]),
        mesh=mesh,
        in_specs=placed,
        out_specs=P(("groups", "blk"), None),
        check_vma=False,
    )
```

```python
import functools

import jax
import jax.numpy as jnp
from jax import lax
from jax.experimental import pallas as pl
from jax.experimental.pallas import tpu as pltpu
from jax.sharding import PartitionSpec as P

MESH = pl.DeviceIdType.MESH
SPAN = 5
REACH = 2
NEAR = 4


def place(offset, slot):
    return {1: 0, 2: 4, -1: 6, -2: 9}[offset] + slot


OUTER_SENDS = (
    (3, 2, place(2, 1)),
    (2, 2, place(2, 2)),
    (1, -1, place(-1, 3)),
    (0, -1, place(-1, 4)),
    (4, 2, place(2, 0)),
)
INNER_SENDS = (
    (2, 1, place(1, 2)),
    (1, 1, place(1, 3)),
    (4, 1, place(1, 0)),
    (0, -2, place(-2, 4)),
    (3, 1, place(1, 1)),
)
OUTER_STEPS = ((2, 2), (-2, 2), (-1, 1), (-2, 3), (-1, 2), (-1, 3), (2, 0), (-2, 4), (-1, 4), (2, 1))
INNER_STEPS = ((1, 2), (2, 1), (1, 3), (2, 2), (1, 0), (-2, 2), (-2, 3), (1, 1), (2, 0), (-2, 4))
OUTER_FORWARDS = {
    (-1, 2): ((1, place(-2, 2)),),
    (-1, 3): ((1, place(-2, 3)),),
    (-1, 4): ((1, place(-2, 4)),),
}
INNER_FORWARDS = {
    (1, 2): ((3, place(-2, 2)), (-1, place(2, 2))),
    (2, 1): ((3, place(-1, 1)),),
    (1, 3): ((3, place(-2, 3)),),
    (2, 2): ((3, place(-1, 2)),),
    (1, 0): ((-1, place(2, 0)),),
    (1, 1): ((-1, place(2, 1)),),
}
COMPLETE = {1: (4, 3), 3: (0, 4), 5: (1, 0), 8: (2, 1), 9: (3, 2)}


def body(
    count,
    width,
    flow_ref,
    occ_ref,
    out_ref,
    own,
    high,
    low,
    recv,
    acc,
    right_high,
    right_low,
    parts,
    load_sem,
    send_sem,
    recv_sem,
    part_send_sem,
    part_recv_sem,
):
    me = lax.axis_index("blk")
    spot = lax.rem(me, 4)
    outer = jnp.logical_or(spot == 0, spot == 3)
    sign = jnp.where(spot < 2, 1, -1)

    def pick(a, b):
        return a if isinstance(a, int) and a == b else jnp.where(outer, a, b)

    def peer(offset):
        return {"blk": lax.rem(me + sign * offset + count, count)}

    def absolute(slot):
        return REACH + sign * (slot - REACH)

    def columns(slot):
        return pl.ds(pl.multiple_of(absolute(slot) * width, width), width)

    def load(slot):
        return pltpu.make_async_copy(flow_ref.at[:, columns(slot)], own.at[slot], load_sem.at[slot])

    def remote(source, target, where, sem):
        return pltpu.make_async_remote_copy(
            src_ref=source,
            dst_ref=recv.at[where],
            send_sem=send_sem.at[sem],
            recv_sem=recv_sem.at[where],
            device_id=target,
            device_id_type=MESH,
        )

    own_slots = [pick(OUTER_SENDS[t][0], INNER_SENDS[t][0]) for t in range(SPAN)]
    for t in range(SPAN):
        load(own_slots[t]).start()

    barrier = pltpu.get_barrier_semaphore()
    for distance in range(1, NEAR + 1):
        for offset in (distance, -distance):
            pl.semaphore_signal(barrier, inc=1, device_id=peer(offset), device_id_type=MESH)
    rows = 64

    def prepare(slot):
        load(slot).wait()
        factor = occ_ref[0, absolute(slot)].astype(jnp.float32)

        @pl.loop(0, width // rows)
        def _(r):
            at = pl.ds(pl.multiple_of(r * rows, rows), rows)
            masked = own[slot, at, :] * factor
            own[slot, at, :] = masked
            top = masked.astype(jnp.bfloat16)
            high[slot, at, :] = top
            low[slot, at, :] = (masked - top.astype(jnp.float32)).astype(jnp.bfloat16)

    def send(t):
        source, offset, where = (pick(a, b) for a, b in zip(OUTER_SENDS[t], INNER_SENDS[t]))
        return remote(own.at[source], peer(offset), where, t)

    def local_send(q):
        return remote(own.at[pick(q + 1, q)], peer(pick(1, -1)), pick(place(-1, q + 1), place(1, q)), SPAN + q)

    for t in range(SPAN):
        prepare(own_slots[t])
        if t == 0:
            pl.semaphore_wait(barrier, 2 * NEAR)
        send(t).start()
    for q in range(SPAN - 1):
        local_send(q).start()

    half = width // 2

    def multiply(left, get_high, get_low, out, first):
        @pl.loop(0, 2)
        def _(c):
            at = pl.ds(pl.multiple_of(c * half, half), half)
            term = functools.partial(jnp.dot, preferred_element_type=jnp.float32)
            total = term(high[left], get_high(at))
            total += term(high[left], get_low(at)) + term(low[left], get_high(at))
            if first:
                acc[out, :, at] = total
            else:
                acc[out, :, at] += total

    @pl.loop(0, SPAN)
    def _(slot):
        multiply(REACH, lambda at: high[slot, :, at], lambda at: low[slot, :, at], slot, True)

    def arrived(where):
        remote(recv.at[where], peer(1), where, 0).wait_recv()

    def add(where, left, out):
        @pl.loop(0, width // rows)
        def _(r):
            at = pl.ds(pl.multiple_of(r * rows, rows), rows)
            value = recv[where, at, :]
            top = value.astype(jnp.bfloat16)
            right_high[at, :] = top
            right_low[at, :] = (value - top.astype(jnp.float32)).astype(jnp.bfloat16)

        multiply(left, lambda at: right_high[:, at], lambda at: right_low[:, at], out, False)

    @pl.loop(0, SPAN - 1)
    def _(q):
        where = jnp.where(outer, q, place(-1, 1) + q)
        arrived(where)
        add(where, pick(3, 1), jnp.where(outer, q + 1, q))

    def complete(slot):
        factor = occ_ref[0, absolute(slot)].astype(jnp.float32)

        def some(r, total):
            at = pl.ds(pl.multiple_of(r * rows, rows), rows)
            expanded = acc[slot, at, :] * factor
            inflated = expanded * expanded
            acc[slot, at, :] = inflated
            return total + jnp.sum(inflated.reshape(rows // 8, 8, width), axis=0)

        total = lax.fori_loop(0, width // rows, some, jnp.zeros((8, width), jnp.float32))
        parts[NEAR, absolute(slot)] = jnp.sum(total, axis=0, keepdims=True)

    def forwards(table, tile):
        found = []
        order = [(t, f) for t in table for f in table[t]]
        for number, (t, (offset, where)) in enumerate(order):
            if t == tile:
                found.append(remote(recv.at[place(*t)], peer(offset), where, 2 * SPAN - 1 + number))
        return found

    for step in range(10):
        far, near = OUTER_STEPS[step], INNER_STEPS[step]
        where = pick(place(*far), place(*near))
        arrived(where)
        if far in OUTER_FORWARDS:
            @pl.when(outer)
            def _():
                for copy in forwards(OUTER_FORWARDS, far):
                    copy.start()
        if near in INNER_FORWARDS:
            @pl.when(jnp.logical_not(outer))
            def _():
                for copy in forwards(INNER_FORWARDS, near):
                    copy.start()
        add(where, pick(far[0] + REACH, near[0] + REACH), pick(sum(far), sum(near)))
        if step in COMPLETE:
            complete(pick(*COMPLETE[step]))

    def part(offset):
        target = {"blk": lax.rem(me + offset + count, count)}
        needed = pl.ds(max(0, offset), SPAN - abs(offset))
        return pltpu.make_async_remote_copy(
            src_ref=parts.at[NEAR, needed],
            dst_ref=parts.at[NEAR - offset, needed],
            send_sem=part_send_sem.at[NEAR - offset],
            recv_sem=part_recv_sem.at[NEAR - offset],
            device_id=target,
            device_id_type=MESH,
        )

    reaches = [offset for offset in range(-NEAR, NEAR + 1) if offset != 0]
    for offset in reaches:
        part(offset).start()
    for offset in reaches:
        part(offset).wait_recv()
    for slot in range(SPAN):
        total = parts[slot, SPAN - 1]
        for d in range(slot - REACH * 2 + 1, slot + 1):
            total = total + parts[NEAR + d, slot - d]
        scale = jnp.where(total > 1.0, 2.0**-64, 2.0**64)
        factor = width / (total * scale)
        source = absolute(slot)

        @pl.loop(0, width // rows)
        def _(r):
            at = pl.ds(pl.multiple_of(r * rows, rows), rows)
            out_ref[at, slot * width : (slot + 1) * width] = acc[source, at, :] * scale * factor

    for offset in reaches:
        part(offset).wait_send()
    for t in range(SPAN):
        send(t).wait_send()
    for q in range(SPAN - 1):
        local_send(q).wait_send()

    @pl.when(outer)
    def _():
        for tile in OUTER_FORWARDS:
            for copy in forwards(OUTER_FORWARDS, tile):
                copy.wait_send()

    @pl.when(jnp.logical_not(outer))
    def _():
        for tile in INNER_FORWARDS:
            for copy in forwards(INNER_FORWARDS, tile):
                copy.wait_send()


def per_device(count, flow, occupancy):
    width = flow.shape[0]
    tile = (width, width)
    places = 14
    return pl.pallas_call(
        functools.partial(body, count, width),
        out_shape=jax.ShapeDtypeStruct(flow.shape, jnp.float32),
        in_specs=[
            pl.BlockSpec(memory_space=pl.ANY),
            pl.BlockSpec(memory_space=pltpu.SMEM),
        ],
        out_specs=pl.BlockSpec(memory_space=pltpu.VMEM),
        scratch_shapes=[
            pltpu.VMEM((SPAN, *tile), jnp.float32),
            pltpu.VMEM((SPAN, *tile), jnp.bfloat16),
            pltpu.VMEM((SPAN, *tile), jnp.bfloat16),
            pltpu.VMEM((places, *tile), jnp.float32),
            pltpu.VMEM((SPAN, *tile), jnp.float32),
            pltpu.VMEM(tile, jnp.bfloat16),
            pltpu.VMEM(tile, jnp.bfloat16),
            pltpu.VMEM((2 * NEAR + 1, SPAN, 1, width), jnp.float32),
            pltpu.SemaphoreType.DMA((SPAN,)),
            pltpu.SemaphoreType.DMA((2 * SPAN - 1 + 8,)),
            pltpu.SemaphoreType.DMA((places,)),
            pltpu.SemaphoreType.DMA((2 * NEAR + 1,)),
            pltpu.SemaphoreType.DMA((2 * NEAR + 1,)),
        ],
        compiler_params=pltpu.CompilerParams(
            collective_id=0, has_side_effects=True, vmem_limit_bytes=48 * 1024 * 1024
        ),
        name="expand",
    )(flow, occupancy)


def solution(mesh):
    placed = (P(("groups", "blk"), None), P(("groups", "blk"), None))
    return jax.shard_map(
        functools.partial(per_device, mesh.shape["blk"]),
        mesh=mesh,
        in_specs=placed,
        out_specs=P(("groups", "blk"), None),
        check_vma=False,
    )
```

```python
import functools

import jax
import jax.numpy as jnp
from jax import lax
from jax.experimental import pallas as pl
from jax.experimental.pallas import tpu as pltpu
from jax.sharding import PartitionSpec as P

MESH = pl.DeviceIdType.MESH
SPAN = 5
REACH = 2
NEAR = 4


def place(offset, slot):
    return {1: 0, 2: 4, -1: 6, -2: 9}[offset] + slot


OUTER_SENDS = (
    (3, 2, place(2, 1)),
    (2, 2, place(2, 2)),
    (1, -1, place(-1, 3)),
    (0, -1, place(-1, 4)),
    (4, 2, place(2, 0)),
)
INNER_SENDS = (
    (2, 1, place(1, 2)),
    (1, 1, place(1, 3)),
    (4, 1, place(1, 0)),
    (0, -2, place(-2, 4)),
    (3, 1, place(1, 1)),
)
OUTER_STEPS = ((2, 2), (-2, 2), (-1, 1), (-2, 3), (-1, 2), (-1, 3), (2, 0), (-1, 4), (-2, 4), (2, 1))
INNER_STEPS = ((1, 2), (2, 1), (1, 3), (2, 2), (1, 0), (-2, 2), (-2, 3), (-2, 4), (1, 1), (2, 0))
OUTER_FORWARDS = {
    (-1, 2): ((1, place(-2, 2)),),
    (-1, 3): ((1, place(-2, 3)),),
    (-1, 4): ((1, place(-2, 4)),),
}
INNER_FORWARDS = {
    (1, 2): ((3, place(-2, 2)), (-1, place(2, 2))),
    (2, 1): ((3, place(-1, 1)),),
    (1, 3): ((3, place(-2, 3)),),
    (2, 2): ((3, place(-1, 2)),),
    (1, 0): ((-1, place(2, 0)),),
    (1, 1): ((-1, place(2, 1)),),
}
COMPLETE = {1: (4, 3), 3: (0, 4), 5: (1, 0), 8: (2, 1), 9: (3, 2)}


def body(
    count,
    width,
    flow_ref,
    occ_ref,
    out_ref,
    own,
    high,
    low,
    recv,
    acc,
    right_high,
    right_low,
    parts,
    load_sem,
    send_sem,
    recv_sem,
    part_send_sem,
    part_recv_sem,
):
    me = lax.axis_index("blk")
    spot = lax.rem(me, 4)
    outer = jnp.logical_or(spot == 0, spot == 3)
    sign = jnp.where(spot < 2, 1, -1)

    def pick(a, b):
        return a if isinstance(a, int) and a == b else jnp.where(outer, a, b)

    def peer(offset):
        return {"blk": lax.rem(me + sign * offset + count, count)}

    def absolute(slot):
        return REACH + sign * (slot - REACH)

    def columns(slot):
        return pl.ds(pl.multiple_of(absolute(slot) * width, width), width)

    def load(slot):
        return pltpu.make_async_copy(flow_ref.at[:, columns(slot)], own.at[slot], load_sem.at[slot])

    def remote(source, target, where, sem):
        return pltpu.make_async_remote_copy(
            src_ref=source,
            dst_ref=recv.at[where],
            send_sem=send_sem.at[sem],
            recv_sem=recv_sem.at[where],
            device_id=target,
            device_id_type=MESH,
        )

    own_slots = [pick(OUTER_SENDS[t][0], INNER_SENDS[t][0]) for t in range(SPAN)]
    for t in range(SPAN):
        load(own_slots[t]).start()

    barrier = pltpu.get_barrier_semaphore()
    for distance in range(1, NEAR + 1):
        for offset in (distance, -distance):
            pl.semaphore_signal(barrier, inc=1, device_id=peer(offset), device_id_type=MESH)
    rows = 64

    def prepare(slot):
        load(slot).wait()
        factor = occ_ref[0, absolute(slot)].astype(jnp.float32)

        @pl.loop(0, width // rows)
        def _(r):
            at = pl.ds(pl.multiple_of(r * rows, rows), rows)
            masked = own[slot, at, :] * factor
            own[slot, at, :] = masked
            top = masked.astype(jnp.bfloat16)
            high[slot, at, :] = top
            low[slot, at, :] = (masked - top.astype(jnp.float32)).astype(jnp.bfloat16)

    def send(t):
        source, offset, where = (pick(a, b) for a, b in zip(OUTER_SENDS[t], INNER_SENDS[t]))
        return remote(own.at[source], peer(offset), where, t)

    def local_send(q):
        return remote(own.at[pick(q + 1, q)], peer(pick(1, -1)), pick(place(-1, q + 1), place(1, q)), SPAN + q)

    for t in range(SPAN):
        prepare(own_slots[t])
        if t == 0:
            pl.semaphore_wait(barrier, 2 * NEAR)
        send(t).start()
    for q in range(SPAN - 1):
        local_send(q).start()

    half = width // 2

    def multiply(left, get_high, get_low, out, first):
        @pl.loop(0, 2)
        def _(c):
            at = pl.ds(pl.multiple_of(c * half, half), half)
            term = functools.partial(jnp.dot, preferred_element_type=jnp.float32)
            total = term(high[left], get_high(at))
            total += term(high[left], get_low(at)) + term(low[left], get_high(at))
            if first:
                acc[out, :, at] = total
            else:
                acc[out, :, at] += total

    @pl.loop(0, SPAN)
    def _(slot):
        multiply(REACH, lambda at: high[slot, :, at], lambda at: low[slot, :, at], slot, True)

    def arrived(where):
        remote(recv.at[where], peer(1), where, 0).wait_recv()

    def add(where, left, out):
        @pl.loop(0, width // rows)
        def _(r):
            at = pl.ds(pl.multiple_of(r * rows, rows), rows)
            value = recv[where, at, :]
            top = value.astype(jnp.bfloat16)
            right_high[at, :] = top
            right_low[at, :] = (value - top.astype(jnp.float32)).astype(jnp.bfloat16)

        multiply(left, lambda at: right_high[:, at], lambda at: right_low[:, at], out, False)

    @pl.loop(0, SPAN - 1)
    def _(q):
        where = jnp.where(outer, q, place(-1, 1) + q)
        arrived(where)
        add(where, pick(3, 1), jnp.where(outer, q + 1, q))

    def complete(slot):
        factor = occ_ref[0, absolute(slot)].astype(jnp.float32)

        def some(r, total):
            at = pl.ds(pl.multiple_of(r * rows, rows), rows)
            expanded = acc[slot, at, :] * factor
            inflated = expanded * expanded
            acc[slot, at, :] = inflated
            return total + jnp.sum(inflated.reshape(rows // 8, 8, width), axis=0)

        total = lax.fori_loop(0, width // rows, some, jnp.zeros((8, width), jnp.float32))
        parts[NEAR, absolute(slot)] = jnp.sum(total, axis=0, keepdims=True)

    def forwards(table, tile):
        found = []
        order = [(t, f) for t in table for f in table[t]]
        for number, (t, (offset, where)) in enumerate(order):
            if t == tile:
                found.append(remote(recv.at[place(*t)], peer(offset), where, 2 * SPAN - 1 + number))
        return found

    for step in range(10):
        far, near = OUTER_STEPS[step], INNER_STEPS[step]
        where = pick(place(*far), place(*near))
        arrived(where)
        if far in OUTER_FORWARDS:
            @pl.when(outer)
            def _():
                for copy in forwards(OUTER_FORWARDS, far):
                    copy.start()
        if near in INNER_FORWARDS:
            @pl.when(jnp.logical_not(outer))
            def _():
                for copy in forwards(INNER_FORWARDS, near):
                    copy.start()
        add(where, pick(far[0] + REACH, near[0] + REACH), pick(sum(far), sum(near)))
        if step in COMPLETE:
            complete(pick(*COMPLETE[step]))

    def part(offset):
        target = {"blk": lax.rem(me + offset + count, count)}
        needed = pl.ds(max(0, offset), SPAN - abs(offset))
        return pltpu.make_async_remote_copy(
            src_ref=parts.at[NEAR, needed],
            dst_ref=parts.at[NEAR - offset, needed],
            send_sem=part_send_sem.at[NEAR - offset],
            recv_sem=part_recv_sem.at[NEAR - offset],
            device_id=target,
            device_id_type=MESH,
        )

    reaches = [offset for offset in range(-NEAR, NEAR + 1) if offset != 0]
    for offset in reaches:
        part(offset).start()
    for offset in reaches:
        part(offset).wait_recv()
    for slot in range(SPAN):
        total = parts[slot, SPAN - 1]
        for d in range(slot - REACH * 2 + 1, slot + 1):
            total = total + parts[NEAR + d, slot - d]
        scale = jnp.where(total > 1.0, 2.0**-64, 2.0**64)
        factor = width / (total * scale)
        source = absolute(slot)

        @pl.loop(0, width // rows)
        def _(r):
            at = pl.ds(pl.multiple_of(r * rows, rows), rows)
            out_ref[at, slot * width : (slot + 1) * width] = acc[source, at, :] * scale * factor

    for offset in reaches:
        part(offset).wait_send()
    for t in range(SPAN):
        send(t).wait_send()
    for q in range(SPAN - 1):
        local_send(q).wait_send()

    @pl.when(outer)
    def _():
        for tile in OUTER_FORWARDS:
            for copy in forwards(OUTER_FORWARDS, tile):
                copy.wait_send()

    @pl.when(jnp.logical_not(outer))
    def _():
        for tile in INNER_FORWARDS:
            for copy in forwards(INNER_FORWARDS, tile):
                copy.wait_send()


def per_device(count, flow, occupancy):
    width = flow.shape[0]
    tile = (width, width)
    places = 14
    return pl.pallas_call(
        functools.partial(body, count, width),
        out_shape=jax.ShapeDtypeStruct(flow.shape, jnp.float32),
        in_specs=[
            pl.BlockSpec(memory_space=pl.ANY),
            pl.BlockSpec(memory_space=pltpu.SMEM),
        ],
        out_specs=pl.BlockSpec(memory_space=pltpu.VMEM),
        scratch_shapes=[
            pltpu.VMEM((SPAN, *tile), jnp.float32),
            pltpu.VMEM((SPAN, *tile), jnp.bfloat16),
            pltpu.VMEM((SPAN, *tile), jnp.bfloat16),
            pltpu.VMEM((places, *tile), jnp.float32),
            pltpu.VMEM((SPAN, *tile), jnp.float32),
            pltpu.VMEM(tile, jnp.bfloat16),
            pltpu.VMEM(tile, jnp.bfloat16),
            pltpu.VMEM((2 * NEAR + 1, SPAN, 1, width), jnp.float32),
            pltpu.SemaphoreType.DMA((SPAN,)),
            pltpu.SemaphoreType.DMA((2 * SPAN - 1 + 8,)),
            pltpu.SemaphoreType.DMA((places,)),
            pltpu.SemaphoreType.DMA((2 * NEAR + 1,)),
            pltpu.SemaphoreType.DMA((2 * NEAR + 1,)),
        ],
        compiler_params=pltpu.CompilerParams(
            collective_id=0, has_side_effects=True, vmem_limit_bytes=48 * 1024 * 1024
        ),
        name="expand",
    )(flow, occupancy)


def solution(mesh):
    placed = (P(("groups", "blk"), None), P(("groups", "blk"), None))
    return jax.shard_map(
        functools.partial(per_device, mesh.shape["blk"]),
        mesh=mesh,
        in_specs=placed,
        out_specs=P(("groups", "blk"), None),
        check_vma=False,
    )
```
